32 devices in a mesh: tok: 8 (over z, x), head: 4 (over y, core).
Axes of the slice: x: 2, y: 2, z: 4, core: 2. Of those that a mesh axis runs over, the one named last changes fastest.
Arguments:
- queries: bfloat16 [128, 8192], P('tok', 'head'), may hold values from -40 to 40
- keys: bfloat16 [8192, 1024], P('tok', 'head'), may hold values from -13 to 13
- values: bfloat16 [8192, 1024], P('tok', 'head'), may hold values from -6 to 6
- out_grad: bfloat16 [128, 8192], P('head', 'tok'), may hold values from -6 to 6
- out_weight: bfloat16 [8192, 8192], P('head', 'tok'), may hold values from -0.0625 to 0.0625
- frame_end: int32 [128], replicated, may hold values from 1 to 64
Outputs:
- query_grad: float32 [128, 8192], P('tok', 'head')
- key_gradient: float32 [8192, 1024], P('tok', 'head')
- value_gradient: float32 [8192, 1024], P('tok', 'head')
- out_weight_grad: float32 [8192, 8192], P('head', 'tok')
The draws below stay inside these ranges and needn't reach their ends.
All inputs are finite; a program needn't handle non-finite values.
Results may differ from the reference program's by a relative error of at most 0.014.
Values may be sent and summed in bfloat16 or wider, within the bound.
A program may use at most 64 MiB of HBM per device.

```python
import math
import jax
import jax.numpy as jnp
from jax import lax

D = 8192
QUERY_HEADS = 64
KEY_VALUE_HEADS = 8
HEAD_SIZE = 128
FRAME = 128
TQ = 128
VISUAL_TOKENS = 8192
FRAMES = 64


def key_start_index(key):
    sampled_inputs = jax.random.normal(jax.random.fold_in(key, 101), (VISUAL_TOKENS, KEY_VALUE_HEADS * HEAD_SIZE), jnp.float32)
    return jnp.clip(1.5 * sampled_inputs, -6.0, 6.0)


def draw_keys(key, part):
    sampled_inputs = key_start_index(key)
    return sampled_inputs.astype(jnp.bfloat16)


def draw_queries(key, part):
    sampled_inputs = jax.random.normal(jax.random.fold_in(key, 202), (TQ, QUERY_HEADS * HEAD_SIZE), jnp.float32)
    sampled_inputs = jnp.clip(1.5 * sampled_inputs, -6.0, 6.0)
    return sampled_inputs.astype(jnp.bfloat16)


def with_ends(entries, own_key, smallest, top_value):
    dims = entries.shape
    spot = [jax.random.randint(jax.random.fold_in(own_key, axis), (), 0, dims[axis]) for axis in range(len(dims))]
    entries = entries.at[tuple(spot)].set(smallest)
    longest = dims.index(max(dims))
    spot[longest] = (spot[longest] + 1) % dims[longest]
    return entries.at[tuple(spot)].set(top_value)


def raised(result, own_key, source, target, blocks, factor):
    def block_of(axis_at):
        return (jnp.arange(result.shape[axis_at]) // (result.shape[axis_at] // blocks)).reshape((-1,) + (1,) * (result.ndim - 1 - axis_at))

    first = jax.random.permutation(own_key, blocks)[block_of(target)]
    far = (block_of(target) + blocks // 2) % blocks
    return jnp.where((block_of(source) == first) | (block_of(source) == far), factor * result, result)


def level_of(key, extent, pieces, smallest, top_value):
    factor_of = 1.0
    for dim, shards_of in pieces:
        steps = jax.random.uniform(jax.random.fold_in(jax.random.fold_in(key, 6), dim), (shards_of,), jnp.float32, smallest / len(pieces), top_value / len(pieces))
        factor_of = factor_of * jnp.repeat(jnp.exp(steps), extent[dim] // shards_of).reshape((-1,) + (1,) * (len(extent) - 1 - dim))
    return factor_of


def normal_values(stream_key, dims, spread, reach, shards=(), kind=jnp.bfloat16):
    entries = spread * jax.random.normal(stream_key, dims, jnp.float32)
    if shards:
        entries = entries * level_of(stream_key, dims, shards, -0.22, 0.18)
    return jnp.clip(entries, -reach, reach).astype(kind)


def bell_draw_with(own_key, shape, width, most, cuts, heavy, kind=jnp.bfloat16):
    array = width * jax.random.normal(own_key, shape, jnp.float32)
    if cuts:
        array = array * level_of(own_key, shape, cuts, -0.22, 0.18)
    return jnp.clip(raised(array, jax.random.fold_in(own_key, 3), *heavy), -most, most).astype(kind)


def setup_inputs(seed: int = 0) -> dict:
    key_of = jax.random.split(jax.random.key(seed), 7)
    queries = draw_queries(jax.random.fold_in(key_of[6], 71), 0)
    keys = draw_keys(jax.random.fold_in(key_of[6], 71), 0)
    values = normal_values(key_of[2], (VISUAL_TOKENS, KEY_VALUE_HEADS * HEAD_SIZE), 1.0, 6.0, ((0, 8), (1, 4)))
    out_grad = bell_draw_with(key_of[3], (TQ, D), 1.0, 6.0, ((0, 4), (1, 8)), (1, 0, 8, 2.0))
    out_weight = normal_values(key_of[4], (QUERY_HEADS * HEAD_SIZE, D), D ** -0.5, 0.0625, ((0, 4), (1, 8)))
    frame_end = with_ends(jax.random.randint(key_of[5], (TQ,), 1, FRAMES + 1), jax.random.fold_in(key_of[5], 1), 1, FRAMES).astype(jnp.int32)
    return {"queries": queries, "keys": keys, "values": values, "out_grad": out_grad, "out_weight": out_weight, "frame_end": frame_end}


def reference(queries, keys, values, out_grad, out_weight, frame_end):
    score_scale = 1.0 / math.sqrt(HEAD_SIZE)
    heads_per_group = QUERY_HEADS // KEY_VALUE_HEADS
    positions = jnp.arange(VISUAL_TOKENS, dtype=jnp.int32)
    visible = (positions // FRAME)[None, :] < frame_end[:, None]
    head_grad = jnp.dot(out_grad, out_weight.T, preferred_element_type=jnp.float32).astype(jnp.bfloat16)
    query_heads = queries.reshape(TQ, QUERY_HEADS, HEAD_SIZE)
    grad_heads = head_grad.reshape(TQ, QUERY_HEADS, HEAD_SIZE)
    key_head_rows = keys.reshape(VISUAL_TOKENS, KEY_VALUE_HEADS, HEAD_SIZE)
    value_head_rows = values.reshape(VISUAL_TOKENS, KEY_VALUE_HEADS, HEAD_SIZE)

    def single_group(kv_group):
        key_block = lax.dynamic_index_in_dim(key_head_rows, kv_group, 1, False)
        value_block = lax.dynamic_index_in_dim(value_head_rows, kv_group, 1, False)

        def one_head(running, member):
            key_total, value_total = running
            head_number = kv_group * heads_per_group + member
            query_block = lax.dynamic_index_in_dim(query_heads, head_number, 1, False)
            grad_block = lax.dynamic_index_in_dim(grad_heads, head_number, 1, False)
            scores = jnp.dot(query_block, key_block.T, preferred_element_type=jnp.float32) * score_scale
            scores = jnp.where(visible, scores, -jnp.inf)
            row_peak = lax.optimization_barrier(jnp.max(scores, axis=1, keepdims=True))
            exp_scores = jnp.exp(scores - row_peak)
            row_total = lax.optimization_barrier(jnp.sum(exp_scores, axis=1, keepdims=True))
            prob_values = exp_scores / row_total
            prob_low = prob_values.astype(jnp.bfloat16)
            attended_rows = jnp.dot(prob_low, value_block, preferred_element_type=jnp.float32).astype(jnp.bfloat16)
            delta_column = lax.optimization_barrier(jnp.sum(grad_block.astype(jnp.float32) * attended_rows.astype(jnp.float32), axis=1, keepdims=True))
            prob_grad = jnp.dot(grad_block, value_block.T, preferred_element_type=jnp.float32)
            score_grad = (prob_values * (prob_grad - delta_column)).astype(jnp.bfloat16)
            value_total = value_total + jnp.dot(prob_low.T, grad_block, preferred_element_type=jnp.float32)
            key_total = key_total + jnp.dot(score_grad.T, query_block, preferred_element_type=jnp.float32) * score_scale
            query_part = jnp.dot(score_grad, key_block, preferred_element_type=jnp.float32) * score_scale
            return ((key_total, value_total), (query_part, attended_rows))
        empty_rows = jnp.zeros((VISUAL_TOKENS, HEAD_SIZE), jnp.float32)
        (key_total, value_total), (query_pieces, attended_rows) = lax.scan(one_head, (empty_rows, empty_rows), jnp.arange(heads_per_group, dtype=jnp.int32))
        return (key_total, value_total, query_pieces, attended_rows)
    key_gradient_list, value_gradient_list, query_pieces, attended_rows = lax.map(single_group, jnp.arange(KEY_VALUE_HEADS, dtype=jnp.int32))
    key_gradient = jnp.transpose(key_gradient_list, (1, 0, 2)).reshape(VISUAL_TOKENS, KEY_VALUE_HEADS * HEAD_SIZE)
    value_gradient = jnp.transpose(value_gradient_list, (1, 0, 2)).reshape(VISUAL_TOKENS, KEY_VALUE_HEADS * HEAD_SIZE)
    query_grad = jnp.transpose(query_pieces, (2, 0, 1, 3)).reshape(TQ, QUERY_HEADS * HEAD_SIZE)
    attn_out = jnp.transpose(attended_rows, (2, 0, 1, 3)).reshape(TQ, QUERY_HEADS * HEAD_SIZE)
    out_weight_grad = jnp.dot(attn_out.T, out_grad, preferred_element_type=jnp.float32)
    return (query_grad, key_gradient, value_gradient, out_weight_grad)
```

```python
import functools
import math

import jax
import jax.numpy as jnp
from jax import lax
from jax.experimental import pallas as pl
from jax.experimental.pallas import tpu as pltpu
from jax.sharding import PartitionSpec as P

QUERY_HEADS = 64
KEY_VALUE_HEADS = 8
HEAD_SIZE = 128
FRAME = 128
HEADS_PER_GROUP = QUERY_HEADS // KEY_VALUE_HEADS

MASKED = -1e30
LOWEST = -1e29
SCALE = 1.0 / math.sqrt(HEAD_SIZE)
LOG2E = math.log2(math.e)
BF16 = jnp.bfloat16
F32 = jnp.float32
MESH = pl.DeviceIdType.MESH


def dot(left, right, left_dim=1, right_dim=0):
    return lax.dot_general(
        left, right, (((left_dim,), (right_dim,)), ((), ())), preferred_element_type=F32
    )


def send(src, dst, send_sem, recv_sem, peer):
    return pltpu.make_async_remote_copy(
        src_ref=src,
        dst_ref=dst,
        send_sem=send_sem,
        recv_sem=recv_sem,
        device_id=peer,
        device_id_type=MESH,
    )


def kernel(
    tok, head, q_ref, k_hbm, v_hbm, og_ref, ow_hbm, fe_ref,
    dq_ref, dk_ref, dv_ref, att_ref, fg_ref,
    k_ref, v_ref, ow_ref, kt_ref, vt_ref, fg, qall, gsend, grecv, hgall, pbuf, mbuf,
    osend, orecv, ssend, srecv, tall, atall, dqsend, dqrecv,
    load_sem, og_s, og_r, q_s, q_f, q_r, g_s, g_r, h_s, h_f, h_r, o_s, o_r, s_s, s_r,
    t_s, t_f, t_r, a_s, a_f, a_r, dq_s, dq_r,
):
    me = lax.axis_index("tok")
    me_head = lax.axis_index("head")
    pairs = tok // 2
    my_pair = me // 2
    side = me % 2
    partner = me + 1 - 2 * side
    rows, width = q_ref.shape
    key_count = k_ref.shape[0]
    groups = k_ref.shape[1] // HEAD_SIZE
    lanes = HEADS_PER_GROUP * rows

    loads = [
        pltpu.make_async_copy(src, dst, load_sem.at[i])
        for i, (src, dst) in enumerate(((ow_hbm, ow_ref), (k_hbm, k_ref), (v_hbm, v_ref)))
    ]
    for load in loads:
        load.start()
    qall[me] = q_ref[...]
    fg[me_head] = og_ref[...]

    def tok_peer(d):
        return lax.rem(me + d, tok)

    def head_peer(d):
        return lax.rem(me_head + d, head)

    barrier = pltpu.get_barrier_semaphore()

    @pl.loop(1, tok)
    def _(d):
        pl.semaphore_signal(barrier, inc=1, device_id={"tok": tok_peer(d)}, device_id_type=MESH)

    @pl.loop(1, head)
    def _(d):
        pl.semaphore_signal(barrier, inc=1, device_id={"head": head_peer(d)}, device_id_type=MESH)

    pl.semaphore_wait(barrier, tok + head - 2)

    def og_copy(owner, peer):
        return send(fg.at[owner], fg.at[owner], og_s.at[peer], og_r.at[owner], {"head": peer})

    @pl.loop(1, head)
    def _(d):
        og_copy(me_head, head_peer(d)).start()

    class Gather:
        def __init__(self, buf, s, f, r):
            self.buf, self.s, self.f, self.r = buf, s, f, r

        def own(self, peer):
            return send(
                self.buf.at[me], self.buf.at[me], self.s.at[peer], self.r.at[me], {"tok": peer}
            )

        def relay(self, block):
            return send(
                self.buf.at[block], self.buf.at[block], self.f.at[block], self.r.at[block],
                {"tok": partner},
            )

        def arrived(self, block):
            return send(
                self.buf.at[block], self.buf.at[block], self.s.at[block], self.r.at[block],
                {"tok": partner},
            )

        def start(self):
            self.own(partner).start()

            @pl.loop(1, pairs)
            def _(d):
                self.own(2 * lax.rem(my_pair + d, pairs) + side).start()

        def forward(self, d):
            block = 2 * lax.rem(my_pair + d, pairs) + side
            self.arrived(block).wait_recv()
            self.relay(block).start()

        def wait_other(self, d):
            block = 2 * lax.rem(my_pair + d, pairs) + 1 - side
            self.arrived(block).wait_recv()

        def drain(self):
            self.own(partner).wait_send()

            @pl.loop(1, pairs)
            def _(d):
                block = 2 * lax.rem(my_pair + d, pairs) + side
                self.own(block).wait_send()
                self.relay(block).wait_send()

    class Scatter:
        def __init__(self, source, landing, s, r):
            self.source, self.landing, self.s, self.r = source, landing, s, r

        def to(self, peer):
            return send(
                self.source.at[peer], self.landing.at[me], self.s.at[peer], self.r.at[me],
                {"tok": peer},
            )

        def wait_all(self):
            @pl.loop(1, tok)
            def _(d):
                peer = tok_peer(d)
                send(
                    self.source.at[peer], self.landing.at[peer], self.s.at[peer],
                    self.r.at[peer], {"tok": peer},
                ).wait_recv()

        def drain(self):
            @pl.loop(1, tok)
            def _(d):
                self.to(tok_peer(d)).wait_send()

    query_gather = Gather(qall, q_s, q_f, q_r)
    grad_gather = Gather(hgall, h_s, h_f, h_r)
    stat_gather = Gather(tall, t_s, t_f, t_r)
    att_gather = Gather(atall, a_s, a_f, a_r)
    grad_scatter = Scatter(gsend, grecv, g_s, g_r)
    out_scatter = Scatter(osend, orecv, o_s, o_r)
    stat_scatter = Scatter(ssend, srecv, s_s, s_r)
    query_scatter = Scatter(dqsend, dqrecv, dq_s, dq_r)

    query_gather.start()

    for load in loads[1:]:
        load.wait()
    for g in range(groups):
        cols = slice(g * HEAD_SIZE, (g + 1) * HEAD_SIZE)
        kt_ref[g] = k_ref[:, cols].astype(F32).T.astype(BF16)
        vt_ref[g] = v_ref[:, cols].astype(F32).T.astype(BF16)

    loads[0].wait()

    @pl.loop(1, head)
    def _(d):
        peer = head_peer(d)
        send(fg.at[peer], fg.at[peer], og_s.at[peer], og_r.at[peer], {"head": peer}).wait_recv()

    full = fg[...].reshape(tok * rows, fg.shape[2])
    tile = min(256, width)

    @pl.loop(0, width // tile)
    def _(i):
        start = pl.multiple_of(i * tile, tile)
        part = dot(full, ow_ref[pl.ds(start, tile), :], 1, 1).astype(BF16)
        gsend[:, :, pl.ds(start, tile)] = part.reshape(tok, rows, tile)

    grecv[me] = gsend[me]

    @pl.loop(1, tok)
    def _(d):
        grad_scatter.to(tok_peer(d)).start()

    def stacked(buf, pair, g):
        pieces = []
        for one in range(2):
            block = buf[2 * pair + one]
            for h in range(HEADS_PER_GROUP):
                at = (g * HEADS_PER_GROUP + h) * HEAD_SIZE
                pieces.append(block[:, at : at + HEAD_SIZE])
        return jnp.concatenate(pieces, axis=0)

    token = lax.broadcasted_iota(jnp.int32, (key_count, 2 * lanes), 0)
    row8 = lax.broadcasted_iota(jnp.int32, (8, lanes), 0)

    def forward_pair(pair):
        limit = fe_ref[pair] * FRAME - me * key_count
        for g in range(groups):
            cols = slice(g * HEAD_SIZE, (g + 1) * HEAD_SIZE)
            scores = dot(k_ref[:, cols], stacked(qall, pair, g), 1, 1) * (SCALE * LOG2E)
            scores = jnp.where(token < limit, scores, MASKED)
            peak = jnp.maximum(jnp.max(scores, axis=0, keepdims=True), LOWEST)
            powers = jnp.exp2(scores - peak)
            total = jnp.sum(powers, axis=0, keepdims=True)
            low = powers.astype(BF16)
            pbuf[pair, g] = low
            mbuf[pair, g] = peak
            out = dot(vt_ref[g], low).astype(BF16)
            for one in range(2):
                part = slice(one * lanes, (one + 1) * lanes)
                osend[2 * pair + one, g] = out[:, part]
                ssend[2 * pair + one, g] = jnp.where(row8 == 0, peak[:, part], total[:, part])

    forward_pair_of = lambda d: lax.rem(my_pair + d, pairs)
    query_gather.arrived(partner).wait_recv()
    forward_pair(my_pair)
    orecv[me] = osend[me]
    srecv[me] = ssend[me]
    stat_scatter.to(partner).start()
    out_scatter.to(partner).start()
    if pairs > 1:
        query_gather.forward(1)

        @pl.loop(1, pairs)
        def _(d):
            @pl.when(d + 1 < pairs)
            def _():
                query_gather.forward(d + 1)

            query_gather.wait_other(d)
            pair = forward_pair_of(d)
            forward_pair(pair)
            for one in range(2):
                stat_scatter.to(2 * pair + one).start()
                out_scatter.to(2 * pair + one).start()

    grad_scatter.wait_all()
    hgall[me] = jnp.sum(grecv[...].astype(F32), axis=0).astype(BF16)
    grad_gather.start()

    stat_scatter.wait_all()
    out_scatter.wait_all()
    for g in range(groups):
        peaks = [srecv[j, g][0:1] for j in range(tok)]
        totals = [srecv[j, g][1:2] for j in range(tok)]
        peak = functools.reduce(jnp.maximum, peaks)
        weights = [jnp.exp2(one - peak) for one in peaks]
        inverse = 1.0 / functools.reduce(jnp.add, [a * b for a, b in zip(weights, totals)])
        merged = jnp.zeros((HEAD_SIZE, lanes), F32)
        for j in range(tok):
            merged += orecv[j, g].astype(F32) * weights[j]
        merged = (merged * inverse).astype(BF16).astype(F32)
        merged_rows = merged.T
        products = jnp.zeros((1, lanes), F32)
        grad_rows = []
        for h in range(HEADS_PER_GROUP):
            at = (g * HEADS_PER_GROUP + h) * HEAD_SIZE
            atall[me, :, at : at + HEAD_SIZE] = merged_rows[h * rows : (h + 1) * rows].astype(BF16)
            grad_rows.append(hgall[me, :, at : at + HEAD_SIZE].astype(F32))
        grad_t = jnp.concatenate(grad_rows, axis=0).T
        delta = jnp.sum(grad_t * merged, axis=0, keepdims=True)
        tall[me, g] = jnp.where(row8 == 0, peak, jnp.where(row8 == 1, inverse, delta))
    stat_gather.start()
    att_gather.start()

    dk_ref[...] = jnp.zeros_like(dk_ref)
    dv_ref[...] = jnp.zeros_like(dv_ref)

    def backward_pair(pair):
        for g in range(groups):
            cols = slice(g * HEAD_SIZE, (g + 1) * HEAD_SIZE)
            stats = jnp.concatenate([tall[2 * pair, g], tall[2 * pair + 1, g]], axis=1)
            factor = jnp.exp2(mbuf[pair, g] - stats[0:1]) * stats[1:2]
            grads = stacked(hgall, pair, g)
            probs = pbuf[pair, g].astype(F32) * factor
            prob_grad = dot(v_ref[:, cols], grads, 1, 1)
            score_grad = (probs * (prob_grad - stats[2:3])).astype(BF16)
            dv_ref[:, cols] += dot(probs.astype(BF16), grads)
            dk_ref[:, cols] += dot(score_grad, stacked(qall, pair, g)) * SCALE
            query_part = (dot(kt_ref[g], score_grad) * SCALE).astype(BF16)
            for one in range(2):
                dqsend[2 * pair + one, g] = query_part[:, one * lanes : (one + 1) * lanes]

    grad_gather.arrived(partner).wait_recv()
    stat_gather.arrived(partner).wait_recv()
    backward_pair(my_pair)
    dqrecv[me] = dqsend[me]
    query_scatter.to(partner).start()
    if pairs > 1:
        grad_gather.forward(1)
        stat_gather.forward(1)

        @pl.loop(1, pairs)
        def _(d):
            @pl.when(d + 1 < pairs)
            def _():
                grad_gather.forward(d + 1)
                stat_gather.forward(d + 1)

            grad_gather.wait_other(d)
            stat_gather.wait_other(d)
            pair = forward_pair_of(d)
            backward_pair(pair)
            for one in range(2):
                query_scatter.to(2 * pair + one).start()

        @pl.loop(1, pairs)
        def _(d):
            att_gather.forward(d)

        att_gather.arrived(partner).wait_recv()

        @pl.loop(1, pairs)
        def _(d):
            att_gather.wait_other(d)
    else:
        att_gather.arrived(partner).wait_recv()

    fg_ref[...] = fg[...]
    att_ref[...] = atall[...]
    query_scatter.wait_all()
    for g in range(groups):
        merged_rows = jnp.sum(dqrecv[:, g].astype(F32), axis=0).T
        for h in range(HEADS_PER_GROUP):
            at = (g * HEADS_PER_GROUP + h) * HEAD_SIZE
            dq_ref[:, at : at + HEAD_SIZE] = merged_rows[h * rows : (h + 1) * rows]

    @pl.loop(1, head)
    def _(d):
        og_copy(me_head, head_peer(d)).wait_send()

    for gather in (query_gather, grad_gather, stat_gather, att_gather):
        gather.drain()
    for scatter in (grad_scatter, out_scatter, stat_scatter, query_scatter):
        scatter.drain()


def body(tok, head, queries, keys, values, out_grad, out_weight, frame_end):
    rows, width = queries.shape
    key_count, key_width = keys.shape
    groups = key_width // HEAD_SIZE
    depth = out_grad.shape[1]
    lanes = HEADS_PER_GROUP * rows
    ends = jnp.broadcast_to(frame_end.reshape(tok, 1, rows), (tok, HEADS_PER_GROUP, rows))
    ends = ends.reshape(tok // 2, 1, 2 * lanes)
    vmem = pl.BlockSpec(memory_space=pltpu.VMEM)
    hbm = pl.BlockSpec(memory_space=pl.ANY)
    dma = pltpu.SemaphoreType.DMA
    query_grad, key_gradient, value_gradient, attended, full_grad = pl.pallas_call(
        functools.partial(kernel, tok, head),
        out_shape=(
            jax.ShapeDtypeStruct((rows, width), F32),
            jax.ShapeDtypeStruct((key_count, key_width), F32),
            jax.ShapeDtypeStruct((key_count, key_width), F32),
            jax.ShapeDtypeStruct((tok, rows, width), BF16),
            jax.ShapeDtypeStruct((head,) + out_grad.shape, BF16),
        ),
        in_specs=[vmem, hbm, hbm, vmem, hbm, vmem],
        out_specs=(vmem,) * 5,
        scratch_shapes=[
            pltpu.VMEM(keys.shape, BF16),
            pltpu.VMEM(values.shape, BF16),
            pltpu.VMEM(out_weight.shape, BF16),
            pltpu.VMEM((groups, HEAD_SIZE, key_count), BF16),
            pltpu.VMEM((groups, HEAD_SIZE, key_count), BF16),
            pltpu.VMEM((head,) + out_grad.shape, BF16),
            pltpu.VMEM((tok, rows, width), BF16),
            pltpu.VMEM((tok, rows, width), BF16),
            pltpu.VMEM((tok, rows, width), BF16),
            pltpu.VMEM((tok, rows, width), BF16),
            pltpu.VMEM((tok // 2, groups, key_count, 2 * lanes), BF16),
            pltpu.VMEM((tok // 2, groups, 1, 2 * lanes), F32),
            pltpu.VMEM((tok, groups, HEAD_SIZE, lanes), BF16),
            pltpu.VMEM((tok, groups, HEAD_SIZE, lanes), BF16),
            pltpu.VMEM((tok, groups, 8, lanes), F32),
            pltpu.VMEM((tok, groups, 8, lanes), F32),
            pltpu.VMEM((tok, groups, 8, lanes), F32),
            pltpu.VMEM((tok, rows, width), BF16),
            pltpu.VMEM((tok, groups, HEAD_SIZE, lanes), BF16),
            pltpu.VMEM((tok, groups, HEAD_SIZE, lanes), BF16),
            dma((3,)),
            dma((head,)),
            dma((head,)),
        ]
        + [dma((tok,)) for _ in range(20)],
        compiler_params=pltpu.CompilerParams(
            collective_id=0, has_side_effects=True, vmem_limit_bytes=56 * 1024 * 1024
        ),
    )(queries, keys, values, out_grad, out_weight, ends)
    row_count = tok * rows
    out_weight_grad = dot(
        attended.reshape(row_count, width), full_grad.reshape(row_count, depth), 0, 0
    )
    return (query_grad, key_gradient, value_gradient, out_weight_grad)


def solution(mesh):
    placed = (
        P("tok", "head"),
        P("tok", "head"),
        P("tok", "head"),
        P("head", "tok"),
        P("head", "tok"),
        P(),
    )
    return jax.shard_map(
        functools.partial(body, mesh.shape["tok"], mesh.shape["head"]),
        mesh=mesh,
        in_specs=placed,
        out_specs=(P("tok", "head"), P("tok", "head"), P("tok", "head"), P("head", "tok")),
        check_vma=False,
    )
```

```python
import functools
import math

import jax
import jax.numpy as jnp
from jax import lax
from jax.experimental import pallas as pl
from jax.experimental.pallas import tpu as pltpu
from jax.sharding import PartitionSpec as P

QUERY_HEADS = 64
KEY_VALUE_HEADS = 8
HEAD_SIZE = 128
FRAME = 128
HEADS_PER_GROUP = QUERY_HEADS // KEY_VALUE_HEADS

MASKED = -1e30
LOWEST = -1e29
SCALE = 1.0 / math.sqrt(HEAD_SIZE)
LOG2E = math.log2(math.e)
BF16 = jnp.bfloat16
F32 = jnp.float32
MESH = pl.DeviceIdType.MESH


def dot(left, right, left_dim=1, right_dim=0):
    return lax.dot_general(
        left, right, (((left_dim,), (right_dim,)), ((), ())), preferred_element_type=F32
    )


def send(src, dst, send_sem, recv_sem, peer):
    return pltpu.make_async_remote_copy(
        src_ref=src,
        dst_ref=dst,
        send_sem=send_sem,
        recv_sem=recv_sem,
        device_id=peer,
        device_id_type=MESH,
    )


def kernel(
    tok, head, q_ref, k_hbm, v_hbm, og_ref, ow_hbm, fe_ref,
    dq_ref, dk_ref, dv_ref, att_ref, fg_ref,
    k_ref, v_ref, ow_ref, kt_ref, vt_ref, fg, qall, gsend, gx, gsum, grecv, hgall, pbuf, mbuf,
    osend, ox, osum, orecv, ssend, sx, ssum, srecv, tall, atall, dqsend, dqx, dqsum, dqrecv,
    load_sem, og_s, og_r, q_s, q_f, q_r, h_s, h_f, h_r, a_s, a_f, a_r, t_s, t_r,
    g_xs, g_xr, g_s, g_r, o_xs, o_xr, o_s, o_r, s_xs, s_xr, s_s, s_r, dq_xs, dq_xr, dq_s, dq_r,
):
    me = lax.axis_index("tok")
    me_head = lax.axis_index("head")
    pairs = tok // 2
    my_pair = me // 2
    side = me % 2
    partner = me + 1 - 2 * side
    rows, width = q_ref.shape
    key_count = k_ref.shape[0]
    groups = k_ref.shape[1] // HEAD_SIZE
    lanes = HEADS_PER_GROUP * rows

    loads = [
        pltpu.make_async_copy(src, dst, load_sem.at[i])
        for i, (src, dst) in enumerate(((ow_hbm, ow_ref), (k_hbm, k_ref), (v_hbm, v_ref)))
    ]
    for load in loads:
        load.start()
    qall[me] = q_ref[...]
    fg[me_head] = og_ref[...]

    def tok_peer(d):
        return lax.rem(me + d, tok)

    def head_peer(d):
        return lax.rem(me_head + d, head)

    barrier = pltpu.get_barrier_semaphore()

    @pl.loop(1, tok)
    def _(d):
        pl.semaphore_signal(barrier, inc=1, device_id={"tok": tok_peer(d)}, device_id_type=MESH)

    @pl.loop(1, head)
    def _(d):
        pl.semaphore_signal(barrier, inc=1, device_id={"head": head_peer(d)}, device_id_type=MESH)

    pl.semaphore_wait(barrier, tok + head - 2)

    def og_copy(owner, peer):
        return send(fg.at[owner], fg.at[owner], og_s.at[peer], og_r.at[owner], {"head": peer})

    @pl.loop(1, head)
    def _(d):
        og_copy(me_head, head_peer(d)).start()

    class Gather:
        def __init__(self, buf, s, f, r):
            self.buf, self.s, self.f, self.r = buf, s, f, r

        def own(self, peer):
            return send(
                self.buf.at[me], self.buf.at[me], self.s.at[peer], self.r.at[me], {"tok": peer}
            )

        def relay(self, block):
            return send(
                self.buf.at[block], self.buf.at[block], self.f.at[block], self.r.at[block],
                {"tok": partner},
            )

        def arrived(self, block):
            return send(
                self.buf.at[block], self.buf.at[block], self.s.at[block], self.r.at[block],
                {"tok": partner},
            )

        def start(self):
            self.own(partner).start()

            @pl.loop(1, pairs)
            def _(d):
                self.own(2 * lax.rem(my_pair + d, pairs) + side).start()

        def forward(self, d):
            block = 2 * lax.rem(my_pair + d, pairs) + side
            self.arrived(block).wait_recv()
            self.relay(block).start()

        def wait_other(self, d):
            block = 2 * lax.rem(my_pair + d, pairs) + 1 - side
            self.arrived(block).wait_recv()

        def drain(self):
            self.own(partner).wait_send()

            @pl.loop(1, pairs)
            def _(d):
                block = 2 * lax.rem(my_pair + d, pairs) + side
                self.own(block).wait_send()
                self.relay(block).wait_send()

    class Scatter:
        def __init__(self, source, across, summed, landing, xs, xr, s, r):
            self.source, self.across, self.summed, self.landing = source, across, summed, landing
            self.xs, self.xr, self.s, self.r = xs, xr, s, r

        def to_partner(self, pair):
            return send(
                self.source.at[2 * pair + 1 - side], self.across.at[pair],
                self.xs.at[pair], self.xr.at[pair], {"tok": partner},
            )

        def along(self, pair, slot):
            return send(
                self.summed.at[pair], self.landing.at[slot], self.s.at[pair], self.r.at[slot],
                {"tok": 2 * pair + side},
            )

        def wait_all(self):
            @pl.loop(1, pairs)
            def _(d):
                pair = pair_at(d)
                self.along(pair, pair).wait_recv()

        def drain(self):
            @pl.loop(0, pairs)
            def _(d):
                self.to_partner(d).wait_send()

            @pl.loop(1, pairs)
            def _(d):
                self.along(pair_at(d), my_pair).wait_send()

    def pair_at(d):
        return lax.rem(my_pair + d, pairs)

    def stat_copy(owner, peer):
        return send(tall.at[owner], tall.at[owner], t_s.at[peer], t_r.at[owner], {"tok": peer})

    query_gather = Gather(qall, q_s, q_f, q_r)
    grad_gather = Gather(hgall, h_s, h_f, h_r)
    att_gather = Gather(atall, a_s, a_f, a_r)
    grad_scatter = Scatter(gsend, gx, gsum, grecv, g_xs, g_xr, g_s, g_r)
    out_scatter = Scatter(osend, ox, osum, orecv, o_xs, o_xr, o_s, o_r)
    stat_scatter = Scatter(ssend, sx, ssum, srecv, s_xs, s_xr, s_s, s_r)
    query_scatter = Scatter(dqsend, dqx, dqsum, dqrecv, dq_xs, dq_xr, dq_s, dq_r)

    def sum_on(scatter, pair, own):
        scatter.to_partner(pair).wait_recv()
        mine = scatter.source[2 * pair + side].astype(F32)
        both = (mine + scatter.across[pair].astype(F32)).astype(BF16)
        if own:
            scatter.landing[pair] = both
        else:
            scatter.summed[pair] = both
            scatter.along(pair, my_pair).start()

    def merge_on(pair, own):
        stat_scatter.to_partner(pair).wait_recv()
        out_scatter.to_partner(pair).wait_recv()
        for g in range(groups):
            first, second = ssend[2 * pair + side, g], sx[pair, g]
            peak = jnp.maximum(first[0:1], second[0:1])
            w_first, w_second = jnp.exp2(first[0:1] - peak), jnp.exp2(second[0:1] - peak)
            total = first[1:2] * w_first + second[1:2] * w_second
            both = osend[2 * pair + side, g].astype(F32) * w_first
            both = (both + ox[pair, g].astype(F32) * w_second).astype(BF16)
            stat = jnp.where(row8 == 0, peak, total)
            if own:
                orecv[pair, g] = both
                srecv[pair, g] = stat
            else:
                osum[pair, g] = both
                ssum[pair, g] = stat
        if not own:
            stat_scatter.along(pair, my_pair).start()
            out_scatter.along(pair, my_pair).start()

    query_gather.start()

    for load in loads[1:]:
        load.wait()
    for g in range(groups):
        cols = slice(g * HEAD_SIZE, (g + 1) * HEAD_SIZE)
        kt_ref[g] = k_ref[:, cols].astype(F32).T.astype(BF16)
        vt_ref[g] = v_ref[:, cols].astype(F32).T.astype(BF16)

    loads[0].wait()

    @pl.loop(1, head)
    def _(d):
        peer = head_peer(d)
        send(fg.at[peer], fg.at[peer], og_s.at[peer], og_r.at[peer], {"head": peer}).wait_recv()

    full = fg[...].reshape(tok * rows, fg.shape[2])
    tile = min(256, width)

    @pl.loop(0, width // tile)
    def _(i):
        start = pl.multiple_of(i * tile, tile)
        part = dot(full, ow_ref[pl.ds(start, tile), :], 1, 1).astype(BF16)
        gsend[:, :, pl.ds(start, tile)] = part.reshape(tok, rows, tile)

    @pl.loop(0, pairs)
    def _(d):
        grad_scatter.to_partner(pair_at(d)).start()

    def stacked(buf, pair, g):
        pieces = []
        for one in range(2):
            block = buf[2 * pair + one]
            for h in range(HEADS_PER_GROUP):
                at = (g * HEADS_PER_GROUP + h) * HEAD_SIZE
                pieces.append(block[:, at : at + HEAD_SIZE])
        return jnp.concatenate(pieces, axis=0)

    row_count = tok * rows
    token = lax.broadcasted_iota(jnp.int32, (key_count, 2 * lanes), 0).astype(F32)
    ends = jnp.broadcast_to(fe_ref[...].astype(F32), (8, row_count)).astype(BF16)
    lane = lax.broadcasted_iota(jnp.int32, (row_count, 2 * lanes), 1)
    lane_row = (lane // lanes) * rows + lane % rows
    row_index = lax.broadcasted_iota(jnp.int32, (row_count, 2 * lanes), 0)
    row8 = lax.broadcasted_iota(jnp.int32, (8, lanes), 0)

    def forward_pair(pair):
        chosen = (row_index == lane_row + pair * (2 * rows)).astype(F32).astype(BF16)
        limit = dot(ends, chosen)[0:1] * FRAME - (me * key_count).astype(F32)
        for g in range(groups):
            cols = slice(g * HEAD_SIZE, (g + 1) * HEAD_SIZE)
            scores = dot(k_ref[:, cols], stacked(qall, pair, g), 1, 1) * (SCALE * LOG2E)
            scores = jnp.where(token < limit, scores, MASKED)
            peak = jnp.maximum(jnp.max(scores, axis=0, keepdims=True), LOWEST)
            powers = jnp.exp2(scores - peak)
            total = jnp.sum(powers, axis=0, keepdims=True)
            low = powers.astype(BF16)
            pbuf[pair, g] = low
            mbuf[pair, g] = peak
            out = dot(vt_ref[g], low).astype(BF16)
            for one in range(2):
                part = slice(one * lanes, (one + 1) * lanes)
                osend[2 * pair + one, g] = out[:, part]
                ssend[2 * pair + one, g] = jnp.where(row8 == 0, peak[:, part], total[:, part])

    def send_out(pair):
        stat_scatter.to_partner(pair).start()
        out_scatter.to_partner(pair).start()

    def finish_grad():
        grad_scatter.wait_all()
        hgall[me] = jnp.sum(grecv[...].astype(F32), axis=0).astype(BF16)
        grad_gather.start()

    if pairs > 1:
        query_gather.forward(1)
    query_gather.arrived(partner).wait_recv()
    forward_pair(my_pair)
    send_out(my_pair)
    sum_on(grad_scatter, my_pair, True)
    if pairs > 1:

        @pl.loop(1, pairs)
        def _(d):
            sum_on(grad_scatter, pair_at(d), False)

    merge_on(my_pair, True)
    if pairs > 1:

        @pl.loop(1, pairs)
        def _(d):
            @pl.when(d + 1 < pairs)
            def _():
                query_gather.forward(d + 1)

            query_gather.wait_other(d)

            @pl.when(d == pairs - 1)
            def _():
                finish_grad()

            pair = pair_at(d)
            forward_pair(pair)
            send_out(pair)

            @pl.when(d > 1)
            def _():
                merge_on(pair_at(d - 1), False)

        merge_on(pair_at(pairs - 1), False)
    else:
        finish_grad()

    stat_scatter.wait_all()
    out_scatter.wait_all()
    for g in range(groups):
        peaks = [srecv[j, g][0:1] for j in range(pairs)]
        totals = [srecv[j, g][1:2] for j in range(pairs)]
        peak = functools.reduce(jnp.maximum, peaks)
        weights = [jnp.exp2(one - peak) for one in peaks]
        inverse = 1.0 / functools.reduce(jnp.add, [a * b for a, b in zip(weights, totals)])
        merged = jnp.zeros((HEAD_SIZE, lanes), F32)
        for j in range(pairs):
            merged += orecv[j, g].astype(F32) * weights[j]
        merged = (merged * inverse).astype(BF16).astype(F32)
        merged_rows = merged.T
        products = jnp.zeros((1, lanes), F32)
        grad_rows = []
        for h in range(HEADS_PER_GROUP):
            at = (g * HEADS_PER_GROUP + h) * HEAD_SIZE
            atall[me, :, at : at + HEAD_SIZE] = merged_rows[h * rows : (h + 1) * rows].astype(BF16)
            grad_rows.append(hgall[me, :, at : at + HEAD_SIZE].astype(F32))
        grad_t = jnp.concatenate(grad_rows, axis=0).T
        delta = jnp.sum(grad_t * merged, axis=0, keepdims=True)
        tall[me, g] = jnp.where(row8 == 0, peak, jnp.where(row8 == 1, inverse, delta))

    @pl.loop(1, tok)
    def _(d):
        stat_copy(me, tok_peer(d)).start()

    att_gather.start()

    dk_ref[...] = jnp.zeros_like(dk_ref)
    dv_ref[...] = jnp.zeros_like(dv_ref)

    def backward_pair(pair):
        for g in range(groups):
            cols = slice(g * HEAD_SIZE, (g + 1) * HEAD_SIZE)
            stats = jnp.concatenate([tall[2 * pair, g], tall[2 * pair + 1, g]], axis=1)
            factor = jnp.exp2(mbuf[pair, g] - stats[0:1]) * stats[1:2]
            grads = stacked(hgall, pair, g)
            probs = pbuf[pair, g].astype(F32) * factor
            prob_grad = dot(v_ref[:, cols], grads, 1, 1)
            score_grad = (probs * (prob_grad - stats[2:3])).astype(BF16)
            dv_ref[:, cols] += dot(probs.astype(BF16), grads)
            dk_ref[:, cols] += dot(score_grad, stacked(qall, pair, g)) * SCALE
            query_part = (dot(kt_ref[g], score_grad) * SCALE).astype(BF16)
            for one in range(2):
                dqsend[2 * pair + one, g] = query_part[:, one * lanes : (one + 1) * lanes]

    def wait_stat(peer):
        stat_copy(peer, peer).wait_recv()

    if pairs > 1:
        grad_gather.forward(1)
    grad_gather.arrived(partner).wait_recv()
    wait_stat(partner)
    backward_pair(my_pair)
    query_scatter.to_partner(my_pair).start()
    if pairs > 1:

        @pl.loop(1, pairs)
        def _(d):
            @pl.when(d + 1 < pairs)
            def _():
                grad_gather.forward(d + 1)

            grad_gather.wait_other(d)
            pair = pair_at(d)
            wait_stat(2 * pair)
            wait_stat(2 * pair + 1)
            backward_pair(pair)
            query_scatter.to_partner(pair).start()
            att_gather.forward(d)

            @pl.when(d > 1)
            def _():
                sum_on(query_scatter, pair_at(d - 1), False)

        sum_on(query_scatter, pair_at(pairs - 1), False)

        @pl.loop(1, pairs)
        def _(d):
            att_gather.wait_other(d)

    sum_on(query_scatter, my_pair, True)
    att_gather.arrived(partner).wait_recv()
    fg_ref[...] = fg[...]
    att_ref[...] = atall[...]
    query_scatter.wait_all()
    for g in range(groups):
        merged_rows = jnp.sum(dqrecv[:, g].astype(F32), axis=0).T
        for h in range(HEADS_PER_GROUP):
            at = (g * HEADS_PER_GROUP + h) * HEAD_SIZE
            dq_ref[:, at : at + HEAD_SIZE] = merged_rows[h * rows : (h + 1) * rows]

    @pl.loop(1, head)
    def _(d):
        og_copy(me_head, head_peer(d)).wait_send()

    @pl.loop(1, tok)
    def _(d):
        stat_copy(me, tok_peer(d)).wait_send()

    for gather in (query_gather, grad_gather, att_gather):
        gather.drain()
    for scatter in (grad_scatter, out_scatter, stat_scatter, query_scatter):
        scatter.drain()


def finish(dq_in, dk_in, dv_in, att_ref, fg_ref, dq_ref, dk_ref, dv_ref, weight_ref):
    dq_ref[...] = dq_in[...]
    dk_ref[...] = dk_in[...]
    dv_ref[...] = dv_in[...]
    weight_ref[...] = dot(att_ref[...], fg_ref[...], 0, 0)


def body(tok, head, queries, keys, values, out_grad, out_weight, frame_end):
    rows, width = queries.shape
    key_count, key_width = keys.shape
    groups = key_width // HEAD_SIZE
    depth = out_grad.shape[1]
    lanes = HEADS_PER_GROUP * rows
    row_count = tok * rows
    block = pltpu.VMEM((tok, rows, width), BF16)
    half = pltpu.VMEM((tok // 2, rows, width), BF16)
    part = pltpu.VMEM((tok, groups, HEAD_SIZE, lanes), BF16)
    half_part = pltpu.VMEM((tok // 2, groups, HEAD_SIZE, lanes), BF16)
    stat = pltpu.VMEM((tok, groups, 8, lanes), F32)
    half_stat = pltpu.VMEM((tok // 2, groups, 8, lanes), F32)
    vmem = pl.BlockSpec(memory_space=pltpu.VMEM)
    hbm = pl.BlockSpec(memory_space=pl.ANY)
    dma = pltpu.SemaphoreType.DMA
    query_grad, key_gradient, value_gradient, attended, full_grad = pl.pallas_call(
        functools.partial(kernel, tok, head),
        out_shape=(
            jax.ShapeDtypeStruct((rows, width), F32),
            jax.ShapeDtypeStruct((key_count, key_width), F32),
            jax.ShapeDtypeStruct((key_count, key_width), F32),
            jax.ShapeDtypeStruct((tok, rows, width), BF16),
            jax.ShapeDtypeStruct((head,) + out_grad.shape, BF16),
        ),
        in_specs=[vmem, hbm, hbm, vmem, hbm, vmem],
        out_specs=(vmem,) * 5,
        scratch_shapes=[
            pltpu.VMEM(keys.shape, BF16),
            pltpu.VMEM(values.shape, BF16),
            pltpu.VMEM(out_weight.shape, BF16),
            pltpu.VMEM((groups, HEAD_SIZE, key_count), BF16),
            pltpu.VMEM((groups, HEAD_SIZE, key_count), BF16),
            pltpu.VMEM((head,) + out_grad.shape, BF16),
            block,
            block,
            half,
            half,
            half,
            block,
            pltpu.VMEM((tok // 2, groups, key_count, 2 * lanes), BF16),
            pltpu.VMEM((tok // 2, groups, 1, 2 * lanes), F32),
            part,
            half_part,
            half_part,
            half_part,
            stat,
            half_stat,
            half_stat,
            half_stat,
            stat,
            block,
            part,
            half_part,
            half_part,
            half_part,
            dma((3,)),
            dma((head,)),
            dma((head,)),
        ]
        + [dma((tok,)) for _ in range(11)]
        + [dma((tok // 2,)) for _ in range(16)],
        compiler_params=pltpu.CompilerParams(
            collective_id=0, has_side_effects=True, vmem_limit_bytes=56 * 1024 * 1024
        ),
    )(queries, keys, values, out_grad, out_weight, frame_end.reshape(1, row_count))
    tile = min(256, width)
    steps = width // tile
    by_rows = pl.BlockSpec((key_count // steps, key_width), lambda i: (i, 0))
    by_columns = pl.BlockSpec((rows, tile), lambda i: (0, i))
    query_grad, key_gradient, value_gradient, out_weight_grad = pl.pallas_call(
        finish,
        grid=(steps,),
        out_shape=(
            jax.ShapeDtypeStruct((rows, width), F32),
            jax.ShapeDtypeStruct((key_count, key_width), F32),
            jax.ShapeDtypeStruct((key_count, key_width), F32),
            jax.ShapeDtypeStruct((width, depth), F32),
        ),
        in_specs=[
            by_columns,
            by_rows,
            by_rows,
            pl.BlockSpec((row_count, tile), lambda i: (0, i)),
            pl.BlockSpec((row_count, depth), lambda i: (0, 0)),
        ],
        out_specs=(
            by_columns, by_rows, by_rows, pl.BlockSpec((tile, depth), lambda i: (i, 0))
        ),
        compiler_params=pltpu.CompilerParams(vmem_limit_bytes=32 * 1024 * 1024),
    )(
        query_grad,
        key_gradient,
        value_gradient,
        attended.reshape(row_count, width),
        full_grad.reshape(row_count, depth),
    )
    return (query_grad, key_gradient, value_gradient, out_weight_grad)


def solution(mesh):
    placed = (
        P("tok", "head"),
        P("tok", "head"),
        P("tok", "head"),
        P("head", "tok"),
        P("head", "tok"),
        P(),
    )
    return jax.shard_map(
        functools.partial(body, mesh.shape["tok"], mesh.shape["head"]),
        mesh=mesh,
        in_specs=placed,
        out_specs=(P("tok", "head"), P("tok", "head"), P("tok", "head"), P("head", "tok")),
        check_vma=False,
    )
```

```python
import functools
import math

import jax
import jax.numpy as jnp
from jax import lax
from jax.experimental import pallas as pl
from jax.experimental.pallas import tpu as pltpu
from jax.sharding import PartitionSpec as P

QUERY_HEADS = 64
KEY_VALUE_HEADS = 8
HEAD_SIZE = 128
FRAME = 128
HEADS_PER_GROUP = QUERY_HEADS // KEY_VALUE_HEADS

MASKED = -1e30
LOWEST = -1e29
SCALE = 1.0 / math.sqrt(HEAD_SIZE)
LOG2E = math.log2(math.e)
BF16 = jnp.bfloat16
F32 = jnp.float32
MESH = pl.DeviceIdType.MESH


def dot(left, right, left_dim=1, right_dim=0):
    return lax.dot_general(
        left, right, (((left_dim,), (right_dim,)), ((), ())), preferred_element_type=F32
    )


def send(src, dst, send_sem, recv_sem, peer):
    return pltpu.make_async_remote_copy(
        src_ref=src,
        dst_ref=dst,
        send_sem=send_sem,
        recv_sem=recv_sem,
        device_id=peer,
        device_id_type=MESH,
    )


def kernel(
    tok, head, q_ref, k_hbm, v_hbm, og_ref, ow_hbm, fe_ref,
    dq_ref, dk_ref, dv_ref, att_ref, fg_ref,
    k_ref, v_ref, ow_ref, kt_ref, vt_ref, fg, qall, gsend, gx, gsum, grecv, hgall, pbuf, mbuf,
    osend, ox, osum, orecv, ssend, sx, ssum, srecv, tall, atall, dqsend, dqx, dqsum, dqrecv,
    load_sem, og_s, og_r, q_s, q_f, q_r, h_s, h_f, h_r, a_s, a_f, a_r, t_s, t_r,
    g_xs, g_xr, g_s, g_r, o_xs, o_xr, o_s, o_r, s_xs, s_xr, s_s, s_r, dq_xs, dq_xr, dq_s, dq_r,
):
    me = lax.axis_index("tok")
    me_head = lax.axis_index("head")
    pairs = tok // 2
    my_pair = me // 2
    side = me % 2
    partner = me + 1 - 2 * side
    rows, width = q_ref.shape
    key_count = k_ref.shape[0]
    groups = k_ref.shape[1] // HEAD_SIZE
    lanes = HEADS_PER_GROUP * rows

    loads = [
        pltpu.make_async_copy(src, dst, load_sem.at[i])
        for i, (src, dst) in enumerate(((ow_hbm, ow_ref), (k_hbm, k_ref), (v_hbm, v_ref)))
    ]
    for load in loads:
        load.start()
    qall[me] = q_ref[...]
    fg[me_head] = og_ref[...]

    def tok_peer(d):
        return lax.rem(me + d, tok)

    def head_peer(d):
        return lax.rem(me_head + d, head)

    barrier = pltpu.get_barrier_semaphore()

    @pl.loop(1, tok)
    def _(d):
        pl.semaphore_signal(barrier, inc=1, device_id={"tok": tok_peer(d)}, device_id_type=MESH)

    @pl.loop(1, head)
    def _(d):
        pl.semaphore_signal(barrier, inc=1, device_id={"head": head_peer(d)}, device_id_type=MESH)

    pl.semaphore_wait(barrier, tok + head - 2)

    def og_copy(owner, peer):
        return send(fg.at[owner], fg.at[owner], og_s.at[peer], og_r.at[owner], {"head": peer})

    @pl.loop(1, head)
    def _(d):
        og_copy(me_head, head_peer(d)).start()

    class Gather:
        def __init__(self, buf, s, f, r):
            self.buf, self.s, self.f, self.r = buf, s, f, r

        def own(self, peer):
            return send(
                self.buf.at[me], self.buf.at[me], self.s.at[peer], self.r.at[me], {"tok": peer}
            )

        def relay(self, block):
            return send(
                self.buf.at[block], self.buf.at[block], self.f.at[block], self.r.at[block],
                {"tok": partner},
            )

        def arrived(self, block):
            return send(
                self.buf.at[block], self.buf.at[block], self.s.at[block], self.r.at[block],
                {"tok": partner},
            )

        def start(self):
            self.own(partner).start()

            @pl.loop(1, pairs)
            def _(d):
                self.own(2 * lax.rem(my_pair + d, pairs) + side).start()

        def forward(self, d):
            block = 2 * lax.rem(my_pair + d, pairs) + side
            self.arrived(block).wait_recv()
            self.relay(block).start()

        def wait_other(self, d):
            block = 2 * lax.rem(my_pair + d, pairs) + 1 - side
            self.arrived(block).wait_recv()

        def drain(self):
            self.own(partner).wait_send()

            @pl.loop(1, pairs)
            def _(d):
                block = 2 * lax.rem(my_pair + d, pairs) + side
                self.own(block).wait_send()
                self.relay(block).wait_send()

    class Scatter:
        def __init__(self, source, across, summed, landing, xs, xr, s, r):
            self.source, self.across, self.summed, self.landing = source, across, summed, landing
            self.xs, self.xr, self.s, self.r = xs, xr, s, r

        def to_partner(self, pair):
            return send(
                self.source.at[2 * pair + 1 - side], self.across.at[pair],
                self.xs.at[pair], self.xr.at[pair], {"tok": partner},
            )

        def along(self, pair, slot):
            return send(
                self.summed.at[pair], self.landing.at[slot], self.s.at[pair], self.r.at[slot],
                {"tok": 2 * pair + side},
            )

        def wait_all(self):
            @pl.loop(1, pairs)
            def _(d):
                pair = pair_at(d)
                self.along(pair, pair).wait_recv()

        def drain(self):
            @pl.loop(0, pairs)
            def _(d):
                self.to_partner(d).wait_send()

            @pl.loop(1, pairs)
            def _(d):
                self.along(pair_at(d), my_pair).wait_send()

    def pair_at(d):
        return lax.rem(my_pair + d, pairs)

    def stat_copy(owner, peer):
        return send(tall.at[owner], tall.at[owner], t_s.at[peer], t_r.at[owner], {"tok": peer})

    query_gather = Gather(qall, q_s, q_f, q_r)
    grad_gather = Gather(hgall, h_s, h_f, h_r)
    att_gather = Gather(atall, a_s, a_f, a_r)
    grad_scatter = Scatter(gsend, gx, gsum, grecv, g_xs, g_xr, g_s, g_r)
    out_scatter = Scatter(osend, ox, osum, orecv, o_xs, o_xr, o_s, o_r)
    stat_scatter = Scatter(ssend, sx, ssum, srecv, s_xs, s_xr, s_s, s_r)
    query_scatter = Scatter(dqsend, dqx, dqsum, dqrecv, dq_xs, dq_xr, dq_s, dq_r)

    def sum_on(scatter, pair, own):
        scatter.to_partner(pair).wait_recv()
        mine = scatter.source[2 * pair + side].astype(F32)
        both = (mine + scatter.across[pair].astype(F32)).astype(BF16)
        if own:
            scatter.landing[pair] = both
        else:
            scatter.summed[pair] = both
            scatter.along(pair, my_pair).start()

    def merge_on(pair, own):
        stat_scatter.to_partner(pair).wait_recv()
        out_scatter.to_partner(pair).wait_recv()
        for g in range(groups):
            first, second = ssend[2 * pair + side, g], sx[pair, g]
            peak = jnp.maximum(first[0:1], second[0:1])
            w_first, w_second = jnp.exp2(first[0:1] - peak), jnp.exp2(second[0:1] - peak)
            total = first[1:2] * w_first + second[1:2] * w_second
            both = osend[2 * pair + side, g].astype(F32) * w_first
            both = (both + ox[pair, g].astype(F32) * w_second).astype(BF16)
            stat = jnp.where(row8 == 0, peak, total)
            if own:
                orecv[pair, g] = both
                srecv[pair, g] = stat
            else:
                osum[pair, g] = both
                ssum[pair, g] = stat
        if not own:
            stat_scatter.along(pair, my_pair).start()
            out_scatter.along(pair, my_pair).start()

    query_gather.start()

    for load in loads[1:]:
        load.wait()
    for g in range(groups):
        cols = slice(g * HEAD_SIZE, (g + 1) * HEAD_SIZE)
        kt_ref[g] = k_ref[:, cols].astype(F32).T.astype(BF16)
        vt_ref[g] = v_ref[:, cols].astype(F32).T.astype(BF16)

    loads[0].wait()

    @pl.loop(1, head)
    def _(d):
        peer = head_peer(d)
        send(fg.at[peer], fg.at[peer], og_s.at[peer], og_r.at[peer], {"head": peer}).wait_recv()

    full = fg[...].reshape(tok * rows, fg.shape[2])
    tile = min(256, width)

    @pl.loop(0, width // tile)
    def _(i):
        start = pl.multiple_of(i * tile, tile)
        part = dot(full, ow_ref[pl.ds(start, tile), :], 1, 1).astype(BF16)
        gsend[:, :, pl.ds(start, tile)] = part.reshape(tok, rows, tile)

    @pl.loop(0, pairs)
    def _(d):
        grad_scatter.to_partner(pair_at(d)).start()

    def stacked(buf, pair, g):
        pieces = []
        for one in range(2):
            block = buf[2 * pair + one]
            for h in range(HEADS_PER_GROUP):
                at = (g * HEADS_PER_GROUP + h) * HEAD_SIZE
                pieces.append(block[:, at : at + HEAD_SIZE])
        return jnp.concatenate(pieces, axis=0)

    row_count = tok * rows
    token = lax.broadcasted_iota(jnp.int32, (key_count, 2 * lanes), 0).astype(F32)
    ends = jnp.broadcast_to(fe_ref[...].astype(F32), (8, row_count)).astype(BF16)
    lane = lax.broadcasted_iota(jnp.int32, (row_count, 2 * lanes), 1)
    lane_row = (lane // lanes) * rows + lane % rows
    row_index = lax.broadcasted_iota(jnp.int32, (row_count, 2 * lanes), 0)
    row8 = lax.broadcasted_iota(jnp.int32, (8, lanes), 0)

    def forward_pair(pair):
        chosen = (row_index == lane_row + pair * (2 * rows)).astype(F32).astype(BF16)
        limit = dot(ends, chosen)[0:1] * FRAME - (me * key_count).astype(F32)
        for g in range(groups):
            cols = slice(g * HEAD_SIZE, (g + 1) * HEAD_SIZE)
            scores = dot(k_ref[:, cols], stacked(qall, pair, g), 1, 1) * (SCALE * LOG2E)
            scores = jnp.where(token < limit, scores, MASKED)
            peak = jnp.maximum(jnp.max(scores, axis=0, keepdims=True), LOWEST)
            powers = jnp.exp2(scores - peak)
            total = jnp.sum(powers, axis=0, keepdims=True)
            low = powers.astype(BF16)
            pbuf[pair, g] = low
            mbuf[pair, g] = peak
            out = dot(vt_ref[g], low).astype(BF16)
            for one in range(2):
                part = slice(one * lanes, (one + 1) * lanes)
                osend[2 * pair + one, g] = out[:, part]
                ssend[2 * pair + one, g] = jnp.where(row8 == 0, peak[:, part], total[:, part])

    def send_out(pair):
        stat_scatter.to_partner(pair).start()
        out_scatter.to_partner(pair).start()

    def finish_grad():
        grad_scatter.wait_all()
        hgall[me] = jnp.sum(grecv[...].astype(F32), axis=0).astype(BF16)
        grad_gather.start()

    if pairs > 1:
        query_gather.forward(1)
    query_gather.arrived(partner).wait_recv()
    forward_pair(my_pair)
    send_out(my_pair)
    sum_on(grad_scatter, my_pair, True)
    if pairs > 1:

        @pl.loop(1, pairs)
        def _(d):
            sum_on(grad_scatter, pair_at(d), False)

    merge_on(my_pair, True)
    if pairs > 1:

        @pl.loop(1, pairs)
        def _(d):
            @pl.when(d + 1 < pairs)
            def _():
                query_gather.forward(d + 1)

            query_gather.wait_other(d)

            @pl.when(d == pairs - 1)
            def _():
                finish_grad()

            pair = pair_at(d)
            forward_pair(pair)
            send_out(pair)

            @pl.when(d > 1)
            def _():
                merge_on(pair_at(d - 1), False)

        merge_on(pair_at(pairs - 1), False)
    else:
        finish_grad()

    stat_scatter.wait_all()
    out_scatter.wait_all()
    for g in range(groups):
        peaks = [srecv[j, g][0:1] for j in range(pairs)]
        totals = [srecv[j, g][1:2] for j in range(pairs)]
        peak = functools.reduce(jnp.maximum, peaks)
        weights = [jnp.exp2(one - peak) for one in peaks]
        inverse = 1.0 / functools.reduce(jnp.add, [a * b for a, b in zip(weights, totals)])
        merged = jnp.zeros((HEAD_SIZE, lanes), F32)
        for j in range(pairs):
            merged += orecv[j, g].astype(F32) * weights[j]
        merged = (merged * inverse).astype(BF16).astype(F32)
        merged_rows = merged.T
        products = jnp.zeros((1, lanes), F32)
        grad_rows = []
        for h in range(HEADS_PER_GROUP):
            at = (g * HEADS_PER_GROUP + h) * HEAD_SIZE
            atall[me, :, at : at + HEAD_SIZE] = merged_rows[h * rows : (h + 1) * rows].astype(BF16)
            grad_rows.append(hgall[me, :, at : at + HEAD_SIZE].astype(F32))
        grad_t = jnp.concatenate(grad_rows, axis=0).T
        delta = jnp.sum(grad_t * merged, axis=0, keepdims=True)
        tall[me, g] = jnp.where(row8 == 0, peak, jnp.where(row8 == 1, inverse, delta))

    @pl.loop(1, tok)
    def _(d):
        stat_copy(me, tok_peer(d)).start()

    att_gather.start()

    dk_ref[...] = jnp.zeros_like(dk_ref)
    dv_ref[...] = jnp.zeros_like(dv_ref)

    def backward_pair(pair):
        for g in range(groups):
            cols = slice(g * HEAD_SIZE, (g + 1) * HEAD_SIZE)
            stats = jnp.concatenate([tall[2 * pair, g], tall[2 * pair + 1, g]], axis=1)
            factor = jnp.exp2(mbuf[pair, g] - stats[0:1]) * stats[1:2]
            grads = stacked(hgall, pair, g)
            probs = pbuf[pair, g].astype(F32) * factor
            prob_grad = dot(v_ref[:, cols], grads, 1, 1)
            score_grad = (probs * (prob_grad - stats[2:3])).astype(BF16)
            dv_ref[:, cols] += dot(probs.astype(BF16), grads)
            dk_ref[:, cols] += dot(score_grad, stacked(qall, pair, g)) * SCALE
            query_part = (dot(kt_ref[g], score_grad) * SCALE).astype(BF16)
            for one in range(2):
                dqsend[2 * pair + one, g] = query_part[:, one * lanes : (one + 1) * lanes]

    def wait_stat(peer):
        stat_copy(peer, peer).wait_recv()

    if pairs > 1:
        grad_gather.forward(1)
    grad_gather.arrived(partner).wait_recv()
    wait_stat(partner)
    backward_pair(my_pair)
    query_scatter.to_partner(my_pair).start()
    if pairs > 1:

        @pl.loop(1, pairs)
        def _(d):
            @pl.when(d + 1 < pairs)
            def _():
                grad_gather.forward(d + 1)

            grad_gather.wait_other(d)
            pair = pair_at(d)
            wait_stat(2 * pair)
            wait_stat(2 * pair + 1)
            backward_pair(pair)
            query_scatter.to_partner(pair).start()
            att_gather.forward(d)

            @pl.when(d > 1)
            def _():
                sum_on(query_scatter, pair_at(d - 1), False)

        sum_on(query_scatter, pair_at(pairs - 1), False)

        @pl.loop(1, pairs)
        def _(d):
            att_gather.wait_other(d)

    sum_on(query_scatter, my_pair, True)
    att_gather.arrived(partner).wait_recv()
    fg_ref[...] = fg[...]
    att_ref[...] = atall[...]
    query_scatter.wait_all()
    for g in range(groups):
        merged_rows = jnp.sum(dqrecv[:, g].astype(F32), axis=0).T
        for h in range(HEADS_PER_GROUP):
            at = (g * HEADS_PER_GROUP + h) * HEAD_SIZE
            dq_ref[:, at : at + HEAD_SIZE] = merged_rows[h * rows : (h + 1) * rows]

    @pl.loop(1, head)
    def _(d):
        og_copy(me_head, head_peer(d)).wait_send()

    @pl.loop(1, tok)
    def _(d):
        stat_copy(me, tok_peer(d)).wait_send()

    for gather in (query_gather, grad_gather, att_gather):
        gather.drain()
    for scatter in (grad_scatter, out_scatter, stat_scatter, query_scatter):
        scatter.drain()


def finish(dq_in, dk_in, dv_in, att_ref, fg_ref, dq_ref, dk_ref, dv_ref, weight_ref):
    dq_ref[...] = dq_in[...]
    dk_ref[...] = dk_in[...]
    dv_ref[...] = dv_in[...]
    weight_ref[...] = dot(att_ref[...], fg_ref[...], 0, 0)


def body(tok, head, queries, keys, values, out_grad, out_weight, frame_end):
    rows, width = queries.shape
    key_count, key_width = keys.shape
    groups = key_width // HEAD_SIZE
    depth = out_grad.shape[1]
    lanes = HEADS_PER_GROUP * rows
    row_count = tok * rows
    block = pltpu.VMEM((tok, rows, width), BF16)
    half = pltpu.VMEM((tok // 2, rows, width), BF16)
    part = pltpu.VMEM((tok, groups, HEAD_SIZE, lanes), BF16)
    half_part = pltpu.VMEM((tok // 2, groups, HEAD_SIZE, lanes), BF16)
    stat = pltpu.VMEM((tok, groups, 8, lanes), F32)
    half_stat = pltpu.VMEM((tok // 2, groups, 8, lanes), F32)
    vmem = pl.BlockSpec(memory_space=pltpu.VMEM)
    hbm = pl.BlockSpec(memory_space=pl.ANY)
    dma = pltpu.SemaphoreType.DMA
    query_grad, key_gradient, value_gradient, attended, full_grad = pl.pallas_call(
        functools.partial(kernel, tok, head),
        out_shape=(
            jax.ShapeDtypeStruct((rows, width), F32),
            jax.ShapeDtypeStruct((key_count, key_width), F32),
            jax.ShapeDtypeStruct((key_count, key_width), F32),
            jax.ShapeDtypeStruct((tok, rows, width), BF16),
            jax.ShapeDtypeStruct((head,) + out_grad.shape, BF16),
        ),
        in_specs=[vmem, hbm, hbm, vmem, hbm, vmem],
        out_specs=(vmem,) * 5,
        scratch_shapes=[
            pltpu.VMEM(keys.shape, BF16),
            pltpu.VMEM(values.shape, BF16),
            pltpu.VMEM(out_weight.shape, BF16),
            pltpu.VMEM((groups, HEAD_SIZE, key_count), BF16),
            pltpu.VMEM((groups, HEAD_SIZE, key_count), BF16),
            pltpu.VMEM((head,) + out_grad.shape, BF16),
            block,
            block,
            half,
            half,
            half,
            block,
            pltpu.VMEM((tok // 2, groups, key_count, 2 * lanes), BF16),
            pltpu.VMEM((tok // 2, groups, 1, 2 * lanes), F32),
            part,
            half_part,
            half_part,
            half_part,
            stat,
            half_stat,
            half_stat,
            half_stat,
            stat,
            block,
            part,
            half_part,
            half_part,
            half_part,
            dma((3,)),
            dma((head,)),
            dma((head,)),
        ]
        + [dma((tok,)) for _ in range(11)]
        + [dma((tok // 2,)) for _ in range(16)],
        compiler_params=pltpu.CompilerParams(
            collective_id=0, has_side_effects=True, vmem_limit_bytes=56 * 1024 * 1024
        ),
    )(queries, keys, values, out_grad, out_weight, frame_end.reshape(1, row_count))
    tile = min(256, width)
    steps = width // tile
    by_rows = pl.BlockSpec((key_count // steps, key_width), lambda i: (i, 0))
    by_columns = pl.BlockSpec((rows, tile), lambda i: (0, i))
    query_grad, key_gradient, value_gradient, out_weight_grad = pl.pallas_call(
        finish,
        grid=(steps,),
        out_shape=(
            jax.ShapeDtypeStruct((rows, width), F32),
            jax.ShapeDtypeStruct((key_count, key_width), F32),
            jax.ShapeDtypeStruct((key_count, key_width), F32),
            jax.ShapeDtypeStruct((width, depth), F32),
        ),
        in_specs=[
            by_columns,
            by_rows,
            by_rows,
            pl.BlockSpec((row_count, tile), lambda i: (0, i)),
            pl.BlockSpec((row_count, depth), lambda i: (0, 0)),
        ],
        out_specs=(
            by_columns, by_rows, by_rows, pl.BlockSpec((tile, depth), lambda i: (i, 0))
        ),
        compiler_params=pltpu.CompilerParams(vmem_limit_bytes=60 * 1024 * 1024),
    )(
        query_grad,
        key_gradient,
        value_gradient,
        attended.reshape(row_count, width),
        full_grad.reshape(row_count, depth),
    )
    return (query_grad, key_gradient, value_gradient, out_weight_grad)


def solution(mesh):
    placed = (
        P("tok", "head"),
        P("tok", "head"),
        P("tok", "head"),
        P("head", "tok"),
        P("head", "tok"),
        P(),
    )
    return jax.shard_map(
        functools.partial(body, mesh.shape["tok"], mesh.shape["head"]),
        mesh=mesh,
        in_specs=placed,
        out_specs=(P("tok", "head"), P("tok", "head"), P("tok", "head"), P("head", "tok")),
        check_vma=False,
    )
```
